32 devices in a mesh: grp: 4 (over y, x), blk: 8 (over z, core).
Axes of the slice: x: 2, y: 2, z: 4, core: 2. Of those that a mesh axis runs over, the one named last changes fastest.
Arguments:
- matrix: bfloat16 [8192, 8192], P('blk', 'grp')
- panels: bfloat16 [8192, 2048], P('grp', 'blk')
- pattern: int32 [64, 64], replicated, may hold values from 0 to 1, as said below
- pruned: int32 [64, 16], replicated, may hold values from 0 to 1, as said below
- owners: int32 [16], replicated, may hold values from 0 to 15, each once
Outputs:
- owned: float32 [8, 4, 256, 2048], P(None, 'grp', None, 'blk')
The draws below stay inside these ranges and needn't reach their ends.
Inputs may be any that keep to these rules, and one draw needn't show every extreme that they name: `pattern`: 0 or 1; every diagonal block is 1. `pruned`: 0 or 1; block (c, c) is 1 for every window column block c; every block row holds exactly 8 ones. `owners`: each slot once.
All inputs are finite; a program needn't handle non-finite values.
Results may differ from the reference program's by a relative error of at most 0.0003.
Values may be sent and summed in bfloat16 or wider, within the bound.
A program may use at most 128 MiB of HBM per device.

```python
import math
import jax
import jax.numpy as jnp

BS = 128
N = 8192
NB = 64
W = 2048
WB = 16
SUB = 256
N_GRP = 4
N_BLK = 8


def rough_values(key, rows, cols):
    values = jnp.exp(jax.random.uniform(key, (rows, cols), jnp.float32, math.log(0.1), math.log(10.0)))
    scale = 1.0 + 2.0 * jnp.arange(rows, dtype=jnp.float32) / (rows - 1)
    return values * scale[:, None]


def draw_matrix(key, part):
    return rough_values(jax.random.fold_in(key, 11), N, N).astype(jnp.bfloat16)


def draw_panels(key, part):
    return rough_values(jax.random.fold_in(key, 23), N, W).astype(jnp.bfloat16)


def draw_pattern(key, part):
    level_key, entry_key = jax.random.split(jax.random.fold_in(key, 37))
    levels = jax.random.randint(level_key, (1, NB), 15, 66)
    entries = jax.random.randint(entry_key, (NB, NB), 0, 100)
    stored = (entries < levels).astype(jnp.int32)
    diagonal = (jnp.arange(NB)[:, None] == jnp.arange(NB)[None, :]).astype(jnp.int32)
    return jnp.maximum(stored, diagonal)


def draw_pruned(key, part):
    raw = jax.random.randint(jax.random.fold_in(key, 41), (NB, WB), 0, 1048576)
    columns = jnp.arange(WB, dtype=jnp.int32)
    diagonal = (jnp.arange(NB, dtype=jnp.int32)[:, None] == columns[None, :]).astype(jnp.int32)
    scores = raw * WB + columns[None, :] + diagonal * (1048576 * WB)
    order = jnp.argsort(-scores, axis=1)
    ranks = jnp.argsort(order, axis=1)
    return (ranks < WB // 2).astype(jnp.int32)


def setup_inputs(seed: int = 0) -> dict:
    key_of = jax.random.split(jax.random.key(seed), 6)
    return {
        "matrix": draw_matrix(jax.random.fold_in(key_of[5], 71), 0),
        "panels": draw_panels(jax.random.fold_in(key_of[5], 71), 0),
        "pattern": draw_pattern(jax.random.fold_in(key_of[5], 71), 0),
        "pruned": draw_pruned(jax.random.fold_in(key_of[5], 71), 0),
        "owners": jax.random.permutation(key_of[4], WB).astype(jnp.int32),
    }


def reference(matrix, panels, pattern, pruned, owners):
    block_rows = N // BS
    window_blocks = W // BS
    left = (matrix.reshape(block_rows, BS, block_rows, BS) * pattern.astype(matrix.dtype)[:, None, :, None]).reshape(N, N)
    right_mask = pattern[:, :window_blocks].astype(panels.dtype)
    right = (panels.reshape(block_rows, BS, window_blocks, BS) * right_mask[:, None, :, None]).reshape(N, W)
    expanded = jnp.dot(left, right, preferred_element_type=jnp.float32)
    inflated = expanded * expanded
    kept = (inflated.reshape(block_rows, BS, window_blocks, BS) * pruned.astype(inflated.dtype)[:, None, :, None]).reshape(N, W)
    totals = jnp.sum(kept, axis=0)
    normalized = N * kept / totals
    inverse = jnp.zeros((window_blocks,), jnp.int32).at[owners].set(jnp.arange(window_blocks, dtype=jnp.int32))
    arranged = normalized.reshape(N_BLK, N_GRP, SUB, window_blocks, BS)[:, :, :, inverse, :]
    return arranged.reshape(N_BLK, N_GRP, SUB, W)
```

```python
import functools

import jax
import jax.numpy as jnp
from jax import lax
from jax.experimental import pallas as pl
from jax.experimental.pallas import tpu as pltpu
from jax.sharding import PartitionSpec as P

BS = 128
MESH = pl.DeviceIdType.MESH
CHUNKS = 4


def encode(values, ref, rows):
    ref[...] = values


def numbers(ref, rows):
    return ref[...]


def kernel(
    G, B,
    matrix_ref, panel_ref, pattern_ref, pruned_ref, owners_ref,
    out_ref, fac_ref,
    got_ref, own, left, pan, stage, rs, kept, out_stage, mine_tot, tot, inv,
    mat_sem, line_send, line_recv, sib_send, sib_recv, rs_send, rs_recv, out_send, out_recv, tot_send, tot_recv,
):
    grp = lax.axis_index("grp")
    blk = lax.axis_index("blk")
    M = B // 2
    m = lax.div(blk, 2)
    core = lax.rem(blk, 2)
    sib = m * 2 + (1 - core)
    rows, inner = left.shape
    width = panel_ref.shape[1]
    row_blocks, inner_blocks, panel_blocks = rows // BS, inner // BS, width // BS
    piece = rows // G
    piece_blocks = piece // BS
    chunk = inner // CHUNKS
    window_blocks = panel_blocks * B

    load = pltpu.make_async_copy(matrix_ref, left, mat_sem)
    load.start()

    barrier = pltpu.get_barrier_semaphore()

    def greet_blk(j, _):
        pl.semaphore_signal(barrier, inc=1, device_id={"blk": lax.rem(blk + j, B)}, device_id_type=MESH)
        return 0

    def greet_grp(j, _):
        pl.semaphore_signal(barrier, inc=1, device_id={"grp": lax.rem(grp + j, G)}, device_id_type=MESH)
        return 0

    lax.fori_loop(1, B, greet_blk, 0)
    lax.fori_loop(1, G, greet_grp, 0)
    pl.semaphore_wait(barrier, B - 1 + G - 1)

    def mask_panel(kb, _):
        at = pl.ds(pl.multiple_of(kb * BS, BS), BS)
        for cb in range(panel_blocks):
            keep = pattern_ref[grp * inner_blocks + kb, blk * panel_blocks + cb].astype(jnp.float32)
            cols = slice(cb * BS, (cb + 1) * BS)
            pan[blk, at, cols] = panel_ref[at, cols] * jnp.full((BS, BS), keep, jnp.float32).astype(jnp.bfloat16)
        return 0

    lax.fori_loop(0, inner_blocks, mask_panel, 0)

    def part(p, ch):
        return pan.at[p, pl.ds(pl.multiple_of(ch * chunk, chunk), chunk), :]

    def line_copy(src, ch, way):
        p = 2 * src + core
        to = blk + 2 - 4 * way
        return pltpu.make_async_remote_copy(
            src_ref=part(p, ch), dst_ref=part(p, ch),
            send_sem=line_send.at[way, src, ch], recv_sem=line_recv.at[src, ch],
            device_id={"blk": lax.rem(to + B, B)}, device_id_type=MESH,
        )

    def sib_copy(src, ch, c):
        p = 2 * src + c
        return pltpu.make_async_remote_copy(
            src_ref=part(p, ch), dst_ref=part(p, ch),
            send_sem=sib_send.at[src, ch], recv_sem=sib_recv.at[src, ch],
            device_id={"blk": sib}, device_id_type=MESH,
        )

    def rs_copy(p, i):
        return pltpu.make_async_remote_copy(
            src_ref=stage.at[p, i - 1], dst_ref=rs.at[p, i - 1],
            send_sem=rs_send.at[p, i - 1], recv_sem=rs_recv.at[p, i - 1],
            device_id={"grp": lax.rem(grp + i, G)}, device_id_type=MESH,
        )

    def send_own(ch, _):
        @pl.when(m + 1 < M)
        def _():
            line_copy(m, ch, 0).start()

        @pl.when(m > 0)
        def _():
            line_copy(m, ch, 1).start()

        sib_copy(m, ch, core).start()
        return 0

    lax.fori_loop(0, CHUNKS, send_own, 0)

    def invert(s, _):
        def look(c, best):
            return jnp.where(owners_ref[c] == s, c, best)

        inv[s] = lax.fori_loop(0, window_blocks, look, jnp.int32(0))
        return 0

    load.wait()

    def mask_left(rb, _):
        at = pl.ds(pl.multiple_of(rb * BS, BS), BS)
        for kb in range(inner_blocks):
            keep = pattern_ref[blk * row_blocks + rb, grp * inner_blocks + kb].astype(jnp.float32)
            cols = slice(kb * BS, (kb + 1) * BS)
            left[at, cols] = left[at, cols] * jnp.full((BS, BS), keep, jnp.float32).astype(jnp.bfloat16)
        return 0

    lax.fori_loop(0, row_blocks, mask_left, 0)

    def product(p, i):
        at = pl.ds(pl.multiple_of((lax.rem(grp + i, G)) * piece, piece), piece)
        return jnp.dot(left[at, :], pan[p], preferred_element_type=jnp.float32)

    def multiply(p):
        def for_peer(i, _):
            encode(product(p, i), stage.at[p, i - 1], piece)
            rs_copy(p, i).start()
            return 0

        for i in range(1, G):
            for_peer(i, 0)
        mine = product(p, 0)
        for cb in range(panel_blocks):
            kept[p * panel_blocks + cb] = mine[:, cb * BS : (cb + 1) * BS]

    def process(src):
        multiply(2 * src + core)

        def arrive(ch, _):
            sib_copy(src, ch, 1 - core).wait_recv()
            return 0

        lax.fori_loop(0, CHUNKS, arrive, 0)
        multiply(2 * src + 1 - core)

    def finish(src):
        def one(c, _):
            p = 2 * src + c

            def arrive(i, _):
                rs_copy(p, i).wait_recv()
                return 0

            for i in range(1, G):
                arrive(i, 0)
            total = jnp.concatenate([kept[p * panel_blocks + cb] for cb in range(panel_blocks)], axis=1)
            for i in range(1, G):
                message = rs.at[p, i - 1]
                total = total + numbers(message, piece)
            total = total * total
            for cb in range(panel_blocks):
                for rb in range(piece_blocks):
                    keep = pruned_ref[
                        blk * row_blocks + grp * piece_blocks + rb, p * panel_blocks + cb
                    ].astype(jnp.float32)
                    kept[p * panel_blocks + cb, rb * BS : (rb + 1) * BS, :] = (
                        total[rb * BS : (rb + 1) * BS, cb * BS : (cb + 1) * BS] * keep
                    )
            return 0

        lax.fori_loop(0, 2, one, 0)

    def pass_on(d):
        def one(ch, _):
            @pl.when(m - d >= 0)
            def _():
                line_copy(m - d, ch, 0).wait_recv()

                @pl.when(m + 1 < M)
                def _():
                    line_copy(m - d, ch, 0).start()

                sib_copy(m - d, ch, core).start()

            @pl.when(m + d < M)
            def _():
                line_copy(m + d, ch, 1).wait_recv()

                @pl.when(m > 0)
                def _():
                    line_copy(m + d, ch, 1).start()

                sib_copy(m + d, ch, core).start()

            return 0

        lax.fori_loop(0, CHUNKS, one, 0)

    def at_distance(d, work):
        @pl.when(m - d >= 0)
        def _():
            work(m - d)

        @pl.when(m + d < M)
        def _():
            work(m + d)

    process(m)
    lax.fori_loop(0, window_blocks, invert, 0)
    pass_on(1)
    finish(m)
    at_distance(1, process)

    def step(d, _):
        pass_on(d)
        at_distance(d - 1, finish)
        at_distance(d, process)
        return 0

    lax.fori_loop(2, M, step, 0)
    at_distance(M - 1, finish)

    def out_copy(j):
        return pltpu.make_async_remote_copy(
            src_ref=out_stage.at[j - 1], dst_ref=got_ref.at[j - 1],
            send_sem=out_send.at[j - 1], recv_sem=out_recv.at[j - 1],
            device_id={"blk": lax.rem(blk + j, B)}, device_id_type=MESH,
        )

    def in_slot_order(to, ref):
        encode(
            jnp.concatenate([kept[inv[to * panel_blocks + cb]] for cb in range(panel_blocks)], axis=1), ref, piece
        )

    def send_out(j, _):
        in_slot_order(lax.rem(blk + j, B), out_stage.at[j - 1])
        out_copy(j).start()
        return 0

    for j in range(1, B):
        send_out(j, 0)
    in_slot_order(blk, own)

    def add_up(source, message, total):
        values = numbers(message, piece)
        out_ref[source] = values
        return total + jnp.sum(values, axis=0, keepdims=True)

    total = add_up(blk, own, jnp.zeros((1, width), jnp.float32))
    for j in range(1, B):
        out_copy(j).wait_recv()
        total = add_up(lax.rem(blk + B - j, B), got_ref.at[j - 1], total)
    mine_tot[...] = jnp.broadcast_to(total, mine_tot.shape)

    def tot_copy(i):
        return pltpu.make_async_remote_copy(
            src_ref=mine_tot, dst_ref=tot.at[i - 1],
            send_sem=tot_send.at[i - 1], recv_sem=tot_recv.at[i - 1],
            device_id={"grp": lax.rem(grp + i, G)}, device_id_type=MESH,
        )

    for i in range(1, G):
        tot_copy(i).start()
    for i in range(1, G):
        tot_copy(i).wait_recv()
        total = total + tot[i - 1, 0:1, :]
    fac_ref[...] = jnp.broadcast_to(float(rows * B) / total, fac_ref.shape)

    for i in range(1, G):
        tot_copy(i).wait_send()

    def out_left(j, _):
        out_copy(j).wait_send()
        return 0

    for j in range(1, B):
        out_left(j, 0)

    def left_line(src, _):
        def one(ch, _):
            @pl.when((src <= m) & (m + 1 < M))
            def _():
                line_copy(src, ch, 0).wait_send()

            @pl.when((src >= m) & (m > 0))
            def _():
                line_copy(src, ch, 1).wait_send()

            sib_copy(src, ch, core).wait_send()
            return 0

        lax.fori_loop(0, CHUNKS, one, 0)
        return 0

    lax.fori_loop(0, M, left_line, 0)

    def left_rs(p, _):
        def one(i, _):
            rs_copy(p, i).wait_send()
            return 0

        for i in range(1, G):
            one(i, 0)
        return 0

    lax.fori_loop(0, B, left_rs, 0)


def shards(matrix, panels, pattern, pruned, owners):
    B = lax.axis_size("blk")
    G = lax.axis_size("grp")
    rows, inner = matrix.shape
    width = panels.shape[1]
    piece = rows // G
    window_blocks = width * B // BS
    M = B // 2
    dma = pltpu.SemaphoreType.DMA
    vmem = pl.BlockSpec(memory_space=pltpu.VMEM)
    smem = pl.BlockSpec(memory_space=pltpu.SMEM)
    got, fac = pl.pallas_call(
        functools.partial(kernel, G, B),
        out_shape=(
            jax.ShapeDtypeStruct((B, piece, width), jnp.float32),
            jax.ShapeDtypeStruct((8, width), jnp.float32),
        ),
        in_specs=[pl.BlockSpec(memory_space=pl.ANY), vmem, smem, smem, smem],
        out_specs=(vmem, vmem),
        scratch_shapes=[
            pltpu.VMEM((B - 1, piece, width), jnp.float32),
            pltpu.VMEM((piece, width), jnp.float32),
            pltpu.VMEM((rows, inner), jnp.bfloat16),
            pltpu.VMEM((B, inner, width), jnp.bfloat16),
            pltpu.VMEM((B, G - 1, piece, width), jnp.float32),
            pltpu.VMEM((B, G - 1, piece, width), jnp.float32),
            pltpu.VMEM((window_blocks, piece, BS), jnp.float32),
            pltpu.VMEM((B - 1, piece, width), jnp.float32),
            pltpu.VMEM((8, width), jnp.float32),
            pltpu.VMEM((G - 1, 8, width), jnp.float32),
            pltpu.SMEM((window_blocks,), jnp.int32),
            dma(()),
            dma((2, M, CHUNKS)),
            dma((M, CHUNKS)),
            dma((M, CHUNKS)),
            dma((M, CHUNKS)),
            dma((B, G - 1)),
            dma((B, G - 1)),
            dma((B - 1,)),
            dma((B - 1,)),
            dma((G - 1,)),
            dma((G - 1,)),
        ],
        compiler_params=pltpu.CompilerParams(
            collective_id=0, has_side_effects=True, vmem_limit_bytes=58 * 1024 * 1024
        ),
        cost_estimate=pl.CostEstimate(
            flops=2 * rows * inner * width * B, bytes_accessed=8 * 1024 * 1024, transcendentals=0
        ),
        name="expand",
    )(matrix, panels, pattern, pruned, owners)
    owned = got * fac[None, 0:1, :]
    return owned[:, None, :, :]


def solution(mesh):
    in_specs = (P("blk", "grp"), P("grp", "blk"), P(), P(), P())
    out_specs = P(None, "grp", None, "blk")
    return jax.shard_map(shards, mesh=mesh, in_specs=in_specs, out_specs=out_specs, check_vma=False)
```

```python
import functools

import jax
import jax.numpy as jnp
from jax import lax
from jax.experimental import pallas as pl
from jax.experimental.pallas import tpu as pltpu
from jax.sharding import PartitionSpec as P

BS = 128
MESH = pl.DeviceIdType.MESH
CHUNKS = 4


STEPS = 256.0
LIMIT = 32700.0
HALF = 32768
TAIL = 8


def encode(values, ref, rows):
    half = rows // 2
    peak = jnp.max(jnp.abs(values), axis=0, keepdims=True)
    code = jnp.ceil(jnp.log(jnp.clip(peak, 1e-35, 3e38)) * STEPS)
    factor = jnp.exp(code * (-1.0 / STEPS)) * LIMIT
    whole = jnp.clip(jnp.round(values * factor), -32767.0, 32767.0).astype(jnp.int32)
    words = whole[0:half] * (2 * HALF) + (whole[half:rows] + HALF)
    codes = jnp.broadcast_to(code, (TAIL, values.shape[1])).astype(jnp.int32)
    ref[...] = jnp.concatenate([words, codes], axis=0)


def numbers(ref, rows):
    half = rows // 2
    message = ref[...]
    scale = jnp.exp(message[half : half + TAIL].astype(jnp.float32)[0:1, :] * (1.0 / STEPS)) * (1.0 / LIMIT)
    words = message[0:half]
    upper = jnp.right_shift(words, 16).astype(jnp.float32)
    lower = (jnp.bitwise_and(words, 2 * HALF - 1) - HALF).astype(jnp.float32)
    return jnp.concatenate([upper, lower], axis=0) * scale


def kernel(
    G, B,
    matrix_ref, panel_ref, pattern_ref, pruned_ref, owners_ref,
    out_ref, fac_ref,
    got_ref, own, left, pan, stage, rs, kept, out_stage, mine_tot, tot, inv,
    mat_sem, line_send, line_recv, sib_send, sib_recv, rs_send, rs_recv, out_send, out_recv, tot_send, tot_recv,
):
    grp = lax.axis_index("grp")
    blk = lax.axis_index("blk")
    M = B // 2
    m = lax.div(blk, 2)
    core = lax.rem(blk, 2)
    sib = m * 2 + (1 - core)
    rows, inner = left.shape
    width = panel_ref.shape[1]
    row_blocks, inner_blocks, panel_blocks = rows // BS, inner // BS, width // BS
    piece = rows // G
    piece_blocks = piece // BS
    chunk = inner // CHUNKS
    window_blocks = panel_blocks * B

    load = pltpu.make_async_copy(matrix_ref, left, mat_sem)
    load.start()

    barrier = pltpu.get_barrier_semaphore()

    def greet_blk(j, _):
        pl.semaphore_signal(barrier, inc=1, device_id={"blk": lax.rem(blk + j, B)}, device_id_type=MESH)
        return 0

    def greet_grp(j, _):
        pl.semaphore_signal(barrier, inc=1, device_id={"grp": lax.rem(grp + j, G)}, device_id_type=MESH)
        return 0

    lax.fori_loop(1, B, greet_blk, 0)
    lax.fori_loop(1, G, greet_grp, 0)
    pl.semaphore_wait(barrier, B - 1 + G - 1)

    def mask_panel(kb, _):
        at = pl.ds(pl.multiple_of(kb * BS, BS), BS)
        for cb in range(panel_blocks):
            keep = pattern_ref[grp * inner_blocks + kb, blk * panel_blocks + cb].astype(jnp.float32)
            cols = slice(cb * BS, (cb + 1) * BS)
            pan[blk, at, cols] = panel_ref[at, cols] * jnp.full((BS, BS), keep, jnp.float32).astype(jnp.bfloat16)
        return 0

    lax.fori_loop(0, inner_blocks, mask_panel, 0)

    def part(p, ch):
        return pan.at[p, pl.ds(pl.multiple_of(ch * chunk, chunk), chunk), :]

    def line_copy(src, ch, way):
        p = 2 * src + core
        to = blk + 2 - 4 * way
        return pltpu.make_async_remote_copy(
            src_ref=part(p, ch), dst_ref=part(p, ch),
            send_sem=line_send.at[way, src, ch], recv_sem=line_recv.at[src, ch],
            device_id={"blk": lax.rem(to + B, B)}, device_id_type=MESH,
        )

    def sib_copy(src, ch, c):
        p = 2 * src + c
        return pltpu.make_async_remote_copy(
            src_ref=part(p, ch), dst_ref=part(p, ch),
            send_sem=sib_send.at[src, ch], recv_sem=sib_recv.at[src, ch],
            device_id={"blk": sib}, device_id_type=MESH,
        )

    def rs_copy(p, i):
        return pltpu.make_async_remote_copy(
            src_ref=stage.at[p, i - 1], dst_ref=rs.at[p, i - 1],
            send_sem=rs_send.at[p, i - 1], recv_sem=rs_recv.at[p, i - 1],
            device_id={"grp": lax.rem(grp + i, G)}, device_id_type=MESH,
        )

    def send_own(ch, _):
        @pl.when(m + 1 < M)
        def _():
            line_copy(m, ch, 0).start()

        @pl.when(m > 0)
        def _():
            line_copy(m, ch, 1).start()

        sib_copy(m, ch, core).start()
        return 0

    lax.fori_loop(0, CHUNKS, send_own, 0)

    def invert(s, _):
        def look(c, best):
            return jnp.where(owners_ref[c] == s, c, best)

        inv[s] = lax.fori_loop(0, window_blocks, look, jnp.int32(0))
        return 0

    load.wait()

    def mask_left(rb, _):
        at = pl.ds(pl.multiple_of(rb * BS, BS), BS)
        for kb in range(inner_blocks):
            keep = pattern_ref[blk * row_blocks + rb, grp * inner_blocks + kb].astype(jnp.float32)
            cols = slice(kb * BS, (kb + 1) * BS)
            left[at, cols] = left[at, cols] * jnp.full((BS, BS), keep, jnp.float32).astype(jnp.bfloat16)
        return 0

    lax.fori_loop(0, row_blocks, mask_left, 0)

    def product(p, i):
        at = pl.ds(pl.multiple_of((lax.rem(grp + i, G)) * piece, piece), piece)
        return jnp.dot(left[at, :], pan[p], preferred_element_type=jnp.float32)

    def multiply(p):
        def for_peer(i, _):
            encode(product(p, i), stage.at[p, i - 1], piece)
            rs_copy(p, i).start()
            return 0

        for i in range(1, G):
            for_peer(i, 0)
        mine = product(p, 0)
        for cb in range(panel_blocks):
            kept[p * panel_blocks + cb] = mine[:, cb * BS : (cb + 1) * BS]

    def process(src):
        multiply(2 * src + core)

        def arrive(ch, _):
            sib_copy(src, ch, 1 - core).wait_recv()
            return 0

        lax.fori_loop(0, CHUNKS, arrive, 0)
        multiply(2 * src + 1 - core)

    def finish(src):
        def one(c, _):
            p = 2 * src + c

            def arrive(i, _):
                rs_copy(p, i).wait_recv()
                return 0

            for i in range(1, G):
                arrive(i, 0)
            total = jnp.concatenate([kept[p * panel_blocks + cb] for cb in range(panel_blocks)], axis=1)
            for i in range(1, G):
                message = rs.at[p, i - 1]
                total = total + numbers(message, piece)
            total = total * total
            for cb in range(panel_blocks):
                for rb in range(piece_blocks):
                    keep = pruned_ref[
                        blk * row_blocks + grp * piece_blocks + rb, p * panel_blocks + cb
                    ].astype(jnp.float32)
                    kept[p * panel_blocks + cb, rb * BS : (rb + 1) * BS, :] = (
                        total[rb * BS : (rb + 1) * BS, cb * BS : (cb + 1) * BS] * keep
                    )
            return 0

        lax.fori_loop(0, 2, one, 0)

    def pass_on(d):
        def one(ch, _):
            @pl.when(m - d >= 0)
            def _():
                line_copy(m - d, ch, 0).wait_recv()

                @pl.when(m + 1 < M)
                def _():
                    line_copy(m - d, ch, 0).start()

                sib_copy(m - d, ch, core).start()

            @pl.when(m + d < M)
            def _():
                line_copy(m + d, ch, 1).wait_recv()

                @pl.when(m > 0)
                def _():
                    line_copy(m + d, ch, 1).start()

                sib_copy(m + d, ch, core).start()

            return 0

        lax.fori_loop(0, CHUNKS, one, 0)

    def at_distance(d, work):
        @pl.when(m - d >= 0)
        def _():
            work(m - d)

        @pl.when(m + d < M)
        def _():
            work(m + d)

    process(m)
    lax.fori_loop(0, window_blocks, invert, 0)
    pass_on(1)
    finish(m)
    at_distance(1, process)

    def step(d, _):
        pass_on(d)
        at_distance(d - 1, finish)
        at_distance(d, process)
        return 0

    lax.fori_loop(2, M, step, 0)
    at_distance(M - 1, finish)

    def out_copy(j):
        return pltpu.make_async_remote_copy(
            src_ref=out_stage.at[j - 1], dst_ref=got_ref.at[j - 1],
            send_sem=out_send.at[j - 1], recv_sem=out_recv.at[j - 1],
            device_id={"blk": lax.rem(blk + j, B)}, device_id_type=MESH,
        )

    def in_slot_order(to, ref):
        encode(
            jnp.concatenate([kept[inv[to * panel_blocks + cb]] for cb in range(panel_blocks)], axis=1), ref, piece
        )

    def send_out(j, _):
        in_slot_order(lax.rem(blk + j, B), out_stage.at[j - 1])
        out_copy(j).start()
        return 0

    for j in range(1, B):
        send_out(j, 0)
    in_slot_order(blk, own)

    def add_up(source, message, total):
        values = numbers(message, piece)
        out_ref[source] = values
        return total + jnp.sum(values, axis=0, keepdims=True)

    total = add_up(blk, own, jnp.zeros((1, width), jnp.float32))
    for j in range(1, B):
        out_copy(j).wait_recv()
        total = add_up(lax.rem(blk + B - j, B), got_ref.at[j - 1], total)
    mine_tot[...] = jnp.broadcast_to(total, mine_tot.shape)

    def tot_copy(i):
        return pltpu.make_async_remote_copy(
            src_ref=mine_tot, dst_ref=tot.at[i - 1],
            send_sem=tot_send.at[i - 1], recv_sem=tot_recv.at[i - 1],
            device_id={"grp": lax.rem(grp + i, G)}, device_id_type=MESH,
        )

    for i in range(1, G):
        tot_copy(i).start()
    for i in range(1, G):
        tot_copy(i).wait_recv()
        total = total + tot[i - 1, 0:1, :]
    fac_ref[...] = jnp.broadcast_to(float(rows * B) / total, fac_ref.shape)

    for i in range(1, G):
        tot_copy(i).wait_send()

    def out_left(j, _):
        out_copy(j).wait_send()
        return 0

    for j in range(1, B):
        out_left(j, 0)

    def left_line(src, _):
        def one(ch, _):
            @pl.when((src <= m) & (m + 1 < M))
            def _():
                line_copy(src, ch, 0).wait_send()

            @pl.when((src >= m) & (m > 0))
            def _():
                line_copy(src, ch, 1).wait_send()

            sib_copy(src, ch, core).wait_send()
            return 0

        lax.fori_loop(0, CHUNKS, one, 0)
        return 0

    lax.fori_loop(0, M, left_line, 0)

    def left_rs(p, _):
        def one(i, _):
            rs_copy(p, i).wait_send()
            return 0

        for i in range(1, G):
            one(i, 0)
        return 0

    lax.fori_loop(0, B, left_rs, 0)


def shards(matrix, panels, pattern, pruned, owners):
    B = lax.axis_size("blk")
    G = lax.axis_size("grp")
    rows, inner = matrix.shape
    width = panels.shape[1]
    piece = rows // G
    window_blocks = width * B // BS
    M = B // 2
    dma = pltpu.SemaphoreType.DMA
    vmem = pl.BlockSpec(memory_space=pltpu.VMEM)
    smem = pl.BlockSpec(memory_space=pltpu.SMEM)
    got, fac = pl.pallas_call(
        functools.partial(kernel, G, B),
        out_shape=(
            jax.ShapeDtypeStruct((B, piece, width), jnp.float32),
            jax.ShapeDtypeStruct((8, width), jnp.float32),
        ),
        in_specs=[pl.BlockSpec(memory_space=pl.ANY), vmem, smem, smem, smem],
        out_specs=(vmem, vmem),
        scratch_shapes=[
            pltpu.VMEM((B - 1, piece // 2 + TAIL, width), jnp.int32),
            pltpu.VMEM((piece // 2 + TAIL, width), jnp.int32),
            pltpu.VMEM((rows, inner), jnp.bfloat16),
            pltpu.VMEM((B, inner, width), jnp.bfloat16),
            pltpu.VMEM((B, G - 1, piece // 2 + TAIL, width), jnp.int32),
            pltpu.VMEM((B, G - 1, piece // 2 + TAIL, width), jnp.int32),
            pltpu.VMEM((window_blocks, piece, BS), jnp.float32),
            pltpu.VMEM((B - 1, piece // 2 + TAIL, width), jnp.int32),
            pltpu.VMEM((8, width), jnp.float32),
            pltpu.VMEM((G - 1, 8, width), jnp.float32),
            pltpu.SMEM((window_blocks,), jnp.int32),
            dma(()),
            dma((2, M, CHUNKS)),
            dma((M, CHUNKS)),
            dma((M, CHUNKS)),
            dma((M, CHUNKS)),
            dma((B, G - 1)),
            dma((B, G - 1)),
            dma((B - 1,)),
            dma((B - 1,)),
            dma((G - 1,)),
            dma((G - 1,)),
        ],
        compiler_params=pltpu.CompilerParams(
            collective_id=0, has_side_effects=True, vmem_limit_bytes=58 * 1024 * 1024
        ),
        cost_estimate=pl.CostEstimate(
            flops=2 * rows * inner * width * B, bytes_accessed=8 * 1024 * 1024, transcendentals=0
        ),
        name="expand",
    )(matrix, panels, pattern, pruned, owners)
    owned = got * fac[None, 0:1, :]
    return owned[:, None, :, :]


def solution(mesh):
    in_specs = (P("blk", "grp"), P("grp", "blk"), P(), P(), P())
    out_specs = P(None, "grp", None, "blk")
    return jax.shard_map(shards, mesh=mesh, in_specs=in_specs, out_specs=out_specs, check_vma=False)
```
